32 devices in a mesh: grp: 2 (over x), seq: 16 (over z, y, core).
Axes of the slice: x: 2, y: 2, z: 4, core: 2. Of those that a mesh axis runs over, the one named last changes fastest.
Arguments:
- queries: bfloat16 [4096, 64, 128], P(('grp', 'seq')), parts along dimension 0, may hold values from -216 to 216
- window_keys: bfloat16 [4096, 8, 128], P(('grp', 'seq')), parts along dimension 0, may hold values from -6 to 6
- window_values: bfloat16 [4096, 8, 128], P(('grp', 'seq')), parts along dimension 0, may hold values from -6 to 6
- cache_keys: bfloat16 [8192, 8, 128], P(('grp', 'seq')), parts along dimension 0, may hold values from -6 to 6
- cache_values: bfloat16 [8192, 8, 128], P(('grp', 'seq')), parts along dimension 0, may hold values from -6 to 6
- vertical_blocks: int32 [128, 4], P('grp'), parts along dimension 0, may hold values from 0 to 63, as said below
- slash_offsets: int32 [128, 12], P('grp'), parts along dimension 0, may hold values from 0 to 31, as said below
Outputs:
- attended: bfloat16 [4096, 64, 128], P(('grp', 'seq')), parts along dimension 0
The draws below stay inside these ranges and needn't reach their ends.
There are 2 independent parts, one for each index of `grp`. The reference program is written for one: setup_inputs(seed, part) draws one part's arguments, and reference() takes and returns one part's arrays. A program takes and returns all parts, laid end to end along the dimension named above; each array names one. Nothing has to cross between parts.
Inputs may be any that keep to these rules, and one draw needn't show every extreme that they name: `vertical_blocks`: the 4 entries of a head are distinct and lie in 4 different runs of 4 consecutive blocks (block b lies in run b // 4). `slash_offsets`: the 12 entries of a head are distinct, and one of them is 0.
All inputs are finite; a program needn't handle non-finite values.
Results may differ from the reference program's by a relative error of at most 0.0046.
Values may be sent and summed in bfloat16 or wider, within the bound.
A program may use at most 128 MiB of HBM per device.

```python
import math
import jax
import jax.numpy as jnp
from jax import lax

H = 64
KVH = 8
HD = 128
BLOCK = 64
NV = 4
NS = 12
CDEV = 256
S = 2048
NQB = 32
PREV = 4096
PREVB = 64


def window_base(key):
    return jnp.clip(jax.random.normal(key, (S, KVH, HD), jnp.float32), -6.0, 6.0)


def draw_window_keys(key, part):
    base = window_base(key)
    return base.astype(jnp.bfloat16)


def draw_queries(key, part):
    key = jax.random.fold_in(key, 3)
    return jnp.clip(jax.random.normal(key, (S, H, HD), jnp.float32), -6.0, 6.0).astype(jnp.bfloat16)


def force_value(picks, head_pick, column, target):
    head_ids = jnp.arange(H, dtype=jnp.int32)[:, None]
    column_ids = jnp.arange(picks.shape[1], dtype=jnp.int32)[None, :]
    present = jnp.any(picks == target, axis=1, keepdims=True)
    return jnp.where((head_ids == head_pick) & (column_ids == column) & jnp.logical_not(present), target, picks)


def draw_vertical_blocks(key, part):
    key = jax.random.fold_in(key, 11)
    local_count = CDEV // BLOCK
    owner_count = PREVB // local_count
    many = jax.random.split(key, H + 2)
    perms = jax.vmap(lambda member: jax.random.permutation(member, owner_count))(many[:H]).astype(jnp.int32)
    owners = perms[:, :NV]
    locals_drawn = jax.random.randint(many[H], (H, NV), 0, local_count, dtype=jnp.int32)
    chosen_heads = jax.random.randint(many[H + 1], (2,), 0, H, dtype=jnp.int32)
    high_head = chosen_heads[0]
    low_head = (high_head + 1 + chosen_heads[1] % (H - 1)) % H
    head_ids = jnp.arange(H, dtype=jnp.int32)[:, None]
    column_ids = jnp.arange(NV, dtype=jnp.int32)[None, :]
    owners = jnp.where(head_ids == high_head, owner_count - 1 - column_ids, owners)
    owners = jnp.where(head_ids == low_head, column_ids, owners)
    first_col = column_ids == 0
    locals_drawn = jnp.where((head_ids == high_head) & first_col, local_count - 1, locals_drawn)
    locals_drawn = jnp.where((head_ids == low_head) & first_col, 0, locals_drawn)
    return (owners * local_count + locals_drawn).astype(jnp.int32)


def draw_slash_offsets(key, part):
    key = jax.random.fold_in(key, 13)
    many = jax.random.split(key, H + 1)
    perms = jax.vmap(lambda member: jax.random.permutation(member, NQB - 1))(many[:H]).astype(jnp.int32)
    others = perms[:, :NS - 1] + 1
    picks = jnp.concatenate([jnp.zeros((H, 1), jnp.int32), others], axis=1)
    high_head = jax.random.randint(many[H], (), 0, H, dtype=jnp.int32)
    picks = force_value(picks, high_head, NS - 1, NQB - 1)
    return picks.astype(jnp.int32)


def levels(own_key, extent, cuts, low, high):
    loudness, own = 1.0, jax.random.fold_in(own_key, 6)
    for dim, blocks in cuts:
        draws = jnp.exp(jax.random.uniform(jax.random.fold_in(own, dim), (blocks,), jnp.float32, low / len(cuts), high / len(cuts)))
        loudness = loudness * jnp.repeat(draws, extent[dim] // blocks).reshape([-1 if axis == dim else 1 for axis in range(len(extent))])
    return loudness


def scatter_about(stream_key, shape, width, limit, shards=(), kind=jnp.bfloat16):
    values = width * jax.random.normal(stream_key, shape, jnp.float32)
    if shards:
        values = values * levels(stream_key, shape, shards, -0.22, 0.18)
    return jnp.clip(values, -limit, limit).astype(kind)


def setup_inputs(seed: int = 0, part: int = 0) -> dict:
    keys = jax.random.split(jax.random.key(seed), 8)
    own_keys = jax.random.split(jax.random.fold_in(keys[7], part), 8)
    return {
        "queries": draw_queries(jax.random.fold_in(jax.random.fold_in(keys[7], part), 71), part),
        "window_keys": draw_window_keys(jax.random.fold_in(jax.random.fold_in(keys[7], part), 71), part),
        "window_values": scatter_about(own_keys[2], (S, KVH, HD), 1.0, 6.0, ((0, 16),)),
        "cache_keys": scatter_about(own_keys[3], (PREV, KVH, HD), 1.0, 6.0, ((0, 16),)),
        "cache_values": scatter_about(own_keys[4], (PREV, KVH, HD), 1.0, 6.0, ((0, 16),)),
        "vertical_blocks": draw_vertical_blocks(jax.random.fold_in(jax.random.fold_in(keys[7], part), 71), part),
        "slash_offsets": draw_slash_offsets(jax.random.fold_in(jax.random.fold_in(keys[7], part), 71), part),
    }


def attend_head(queries, key_rows, values, column_keys, column_values, offsets):
    head_dim = queries.shape[-1]
    blocks = queries.shape[0] // BLOCK
    per_step = math.gcd(512 // BLOCK, blocks)
    query_blocks = queries.reshape(blocks, BLOCK, head_dim)
    key_blocks = key_rows.reshape(blocks, BLOCK, head_dim)
    value_blocks = values.reshape(blocks, BLOCK, head_dim)
    column_flat = column_keys.reshape(-1, head_dim)
    column_vals = column_values.reshape(-1, head_dim)
    factor = 1.0 / math.sqrt(head_dim)
    places = jnp.arange(BLOCK, dtype=jnp.int32)
    earlier = places[None, :] <= places[:, None]
    open_slash = offsets != 0

    def one_step(first_block):
        block_ids = first_block + jnp.arange(per_step, dtype=jnp.int32)
        sources = block_ids[:, None] - offsets[None, :]
        usable = sources >= 0
        safe_ids = jnp.maximum(sources, 0).astype(jnp.int32)
        query_group = lax.dynamic_slice_in_dim(query_blocks, first_block, per_step, 0)
        slash_keys = key_blocks[safe_ids].reshape(per_step, -1, head_dim)
        slash_values = value_blocks[safe_ids].reshape(per_step, -1, head_dim)
        slash_scores = jnp.einsum('gqd,gkd->gqk', query_group.astype(jnp.float32), slash_keys.astype(jnp.float32)) * factor
        column_scores = jnp.dot(query_group.reshape(-1, head_dim), column_flat.T, preferred_element_type=jnp.float32).reshape(per_step, BLOCK, -1) * factor
        keep = usable[:, None, :, None] & (open_slash[None, None, :, None] | earlier[None, :, None, :])
        keep = keep.reshape(per_step, BLOCK, -1)
        slash_scores = jnp.where(keep, slash_scores, -1e+30)
        highest = jnp.maximum(lax.optimization_barrier(jnp.max(slash_scores, axis=-1)), lax.optimization_barrier(jnp.max(column_scores, axis=-1)))
        slash_weights = jnp.exp(slash_scores - highest[..., None])
        column_weights = jnp.exp(column_scores - highest[..., None])
        total = lax.optimization_barrier(jnp.sum(slash_weights, axis=-1)) + lax.optimization_barrier(jnp.sum(column_weights, axis=-1))
        slash_low = lax.optimization_barrier(slash_weights.astype(jnp.bfloat16))
        column_low = column_weights.astype(jnp.bfloat16)
        mixed = jnp.einsum('gqk,gkd->gqd', slash_low.astype(jnp.float32), slash_values.astype(jnp.float32))
        mixed = mixed + jnp.dot(column_low.reshape(-1, column_low.shape[-1]), column_vals, preferred_element_type=jnp.float32).reshape(per_step, BLOCK, head_dim)
        return (mixed / total[..., None]).astype(jnp.bfloat16)
    starts = jnp.arange(0, blocks, per_step, dtype=jnp.int32)
    result = lax.map(one_step, starts)
    return result.reshape(-1, head_dim)

def reference(queries, window_keys, window_values, cache_keys, cache_values, vertical_blocks, slash_offsets):
    head_count = queries.shape[1]
    group_heads = window_keys.shape[1]
    repeat_count = head_count // group_heads
    head_dim = queries.shape[2]
    cache_kblocks = cache_keys.reshape(-1, BLOCK, group_heads, head_dim)
    cache_vblocks = cache_values.reshape(-1, BLOCK, group_heads, head_dim)

    def per_head(head):
        group_id = head // repeat_count
        key_layer = lax.dynamic_index_in_dim(cache_kblocks, group_id, 2, keepdims=False)
        value_layer = lax.dynamic_index_in_dim(cache_vblocks, group_id, 2, keepdims=False)
        picks = lax.dynamic_index_in_dim(vertical_blocks, head, 0, keepdims=False).astype(jnp.int32)
        column_keys = jnp.take(key_layer, picks, axis=0)
        column_values = jnp.take(value_layer, picks, axis=0)
        offsets = lax.dynamic_index_in_dim(slash_offsets, head, 0, keepdims=False).astype(jnp.int32)
        head_queries = lax.dynamic_index_in_dim(queries, head, 1, keepdims=False)
        head_keys = lax.dynamic_index_in_dim(window_keys, group_id, 1, keepdims=False)
        head_values = lax.dynamic_index_in_dim(window_values, group_id, 1, keepdims=False)
        return attend_head(head_queries, head_keys, head_values, column_keys, column_values, offsets)
    result = lax.map(per_head, jnp.arange(head_count, dtype=jnp.int32))
    return jnp.transpose(result, (1, 0, 2))
```

```python
import functools
import math

import jax
import jax.numpy as jnp
from jax import lax
from jax.experimental import pallas as pl
from jax.experimental.pallas import tpu as pltpu
from jax.sharding import PartitionSpec as P

BLOCK = 64
QUAD = 4
LOG2E = 1.4426950408889634


def attend_block(q, block, first_head, head, offs_ref, vert_ref, w_s, c_s, lane_row, slashes, verts):
    row = first_head + head
    pieces = []
    for c in range(slashes):
        offset = offs_ref[row, c]
        pieces.append((w_s, jnp.maximum(block - offset, 0), offset))
    for c in range(verts):
        pieces.append((c_s, vert_ref[row, c], None))

    def rows(which, piece):
        ref, index, _ = piece
        return ref[which, index]

    factor = LOG2E / math.sqrt(q.shape[-1])
    chunks = [pieces[a : a + QUAD] for a in range(0, len(pieces), QUAD)]
    scores = []
    for chunk in chunks:
        keys = jnp.concatenate([rows(0, piece) for piece in chunk], axis=0)
        s = lax.dot_general(q, keys, (((1,), (1,)), ((), ())), preferred_element_type=jnp.float32)
        if any(piece[2] is not None for piece in chunk):
            lane = lax.broadcasted_iota(jnp.int32, (1, s.shape[1]), 1)
            offsets = jnp.full((1, s.shape[1]), -1, jnp.int32)
            for a, piece in enumerate(chunk):
                if piece[2] is not None:
                    offsets = jnp.where(lane // BLOCK == a, piece[2], offsets)
            limits = jnp.where(offsets > block, -4 * BLOCK, 4 * BLOCK)
            limits = jnp.where(offsets == 0, 0, limits)
            s = jnp.where(lane_row[:, : s.shape[1]] <= limits, s, -1e30)
        scores.append(s)
    top = functools.reduce(jnp.maximum, [jnp.max(s, axis=1, keepdims=True) for s in scores])
    total = None
    mixed = None
    for chunk, s in zip(chunks, scores):
        weights = jnp.exp2((s - top) * factor)
        part = jnp.sum(weights, axis=1, keepdims=True)
        values = jnp.concatenate([rows(1, piece) for piece in chunk], axis=0)
        product = jnp.dot(
            weights.astype(jnp.bfloat16), values, preferred_element_type=jnp.float32
        )
        total = part if total is None else total + part
        mixed = product if mixed is None else mixed + product
    return (mixed / total).astype(jnp.bfloat16)


def kernel(
    n, members, heads, slashes, verts,
    offs_ref, vert_ref, q_in, w_in, c_in, out,
    q_s, w_s, c_s, o_s,
    w_send, w_recv, c_send, c_recv, q_send, q_recv, o_send, o_recv, local_sem,
):
    me = lax.axis_index("seq")
    member = lax.rem(me, members)
    base = me - member
    span = q_in.shape[1]
    first_head = member * heads

    barrier = pltpu.get_barrier_semaphore()

    def greet(k, _):
        pl.semaphore_signal(
            barrier, inc=1, device_id={"seq": lax.rem(me + k, n)},
            device_id_type=pl.DeviceIdType.MESH,
        )
        return 0

    lax.fori_loop(1, n, greet, 0)

    def span_of(index, length):
        return pl.ds(pl.multiple_of(index * length, length), length)

    def blocks_of(index, ref):
        return pl.ds(index * ref.shape[2], ref.shape[2])

    own = [
        pltpu.make_async_copy(w_in.at[member], w_s.at[:, blocks_of(me, w_in)], local_sem.at[0]),
        pltpu.make_async_copy(c_in.at[member], c_s.at[:, blocks_of(me, c_in)], local_sem.at[1]),
        pltpu.make_async_copy(
            q_in.at[pl.ds(first_head, heads)], q_s.at[:, span_of(member, span), :], local_sem.at[2]
        ),
    ]
    for copy in own:
        copy.start()
    pl.semaphore_wait(barrier, n - 1)

    def remote(src, dst, send, recv, peer):
        return pltpu.make_async_remote_copy(
            src_ref=src, dst_ref=dst, send_sem=send, recv_sem=recv,
            device_id={"seq": peer}, device_id_type=pl.DeviceIdType.MESH,
        )

    def w_copy(peer, place):
        return remote(
            w_in.at[lax.rem(peer, members)], w_s.at[:, blocks_of(place, w_in)],
            w_send.at[peer], w_recv.at[place], peer,
        )

    def c_copy(peer, place):
        return remote(
            c_in.at[lax.rem(peer, members)], c_s.at[:, blocks_of(place, c_in)],
            c_send.at[peer], c_recv.at[place], peer,
        )

    def q_copy(head, peer, place):
        return remote(
            q_in.at[peer * heads + head], q_s.at[head, span_of(place, span), :],
            q_send.at[head, peer], q_recv.at[head, place], base + peer,
        )

    def o_copy(head, peer, place):
        return remote(
            o_s.at[head, span_of(peer, span), :], out.at[place * heads + head],
            o_send.at[head, peer], o_recv.at[head, place], base + peer,
        )

    def start_kv(k, _):
        peer = lax.rem(me + k, n)
        w_copy(peer, me).start()
        c_copy(peer, me).start()
        return 0

    lax.fori_loop(1, n, start_kv, 0)

    def start_q(step, _):
        head = step // (members - 1)
        peer = lax.rem(member + 1 + lax.rem(step, members - 1), members)
        q_copy(head, peer, member).start()
        return 0

    lax.fori_loop(0, heads * (members - 1), start_q, 0)

    for copy in own:
        copy.wait()

    def wait_kv(k, _):
        other = lax.rem(me + k, n)
        w_copy(other, other).wait_recv()
        c_copy(other, other).wait_recv()
        return 0

    lax.fori_loop(1, n, wait_kv, 0)

    lane_row = lax.rem(
        lax.broadcasted_iota(jnp.int32, (BLOCK, QUAD * BLOCK), 1), BLOCK
    ) - lax.broadcasted_iota(jnp.int32, (BLOCK, QUAD * BLOCK), 0)
    blocks = members * span // BLOCK
    first_block = (base * span) // BLOCK

    def one_head(head, _):
        def wait_q(k, _):
            other = lax.rem(member + k, members)
            q_copy(head, other, other).wait_recv()
            return 0

        lax.fori_loop(1, members, wait_q, 0)

        def one_block(step, _):
            for half in range(2):
                local = step * 2 + half
                place = pl.ds(pl.multiple_of(local * BLOCK, BLOCK), BLOCK)
                o_s[head, place, :] = attend_block(
                    q_s[head, place, :], first_block + local, first_head, head,
                    offs_ref, vert_ref, w_s, c_s, lane_row, slashes, verts,
                )
            return 0

        lax.fori_loop(0, blocks // 2, one_block, 0)

        def start_o(k, _):
            o_copy(head, lax.rem(member + k, members), member).start()
            return 0

        lax.fori_loop(1, members, start_o, 0)
        pltpu.make_async_copy(
            o_s.at[head, span_of(member, span), :], out.at[first_head + head],
            local_sem.at[3 + head],
        ).start()
        return 0

    lax.fori_loop(0, heads, one_head, 0)

    def finish_kv(k, _):
        peer = lax.rem(me + k, n)
        w_copy(peer, me).wait_send()
        c_copy(peer, me).wait_send()
        return 0

    lax.fori_loop(1, n, finish_kv, 0)

    def finish_head(head, _):
        def each(k, _):
            other = lax.rem(member + k, members)
            q_copy(head, other, member).wait_send()
            o_copy(head, other, member).wait_send()
            o_copy(head, other, other).wait_recv()
            return 0

        lax.fori_loop(1, members, each, 0)
        pltpu.make_async_copy(
            o_s.at[head, span_of(member, span), :], out.at[first_head + head],
            local_sem.at[3 + head],
        ).wait()
        return 0

    lax.fori_loop(0, heads, finish_head, 0)


def body(queries, window_keys, window_values, cache_keys, cache_values, vertical_blocks, slash_offsets):
    n = lax.axis_size("seq")
    span, head_count, dim = queries.shape
    members = window_keys.shape[1]
    cspan = cache_keys.shape[0]
    heads = head_count // members
    q_in = jnp.transpose(queries, (1, 0, 2))

    def by_head(keys, values):
        both = [jnp.transpose(a, (1, 0, 2)).reshape(members, -1, BLOCK, dim) for a in (keys, values)]
        return jnp.stack(both, axis=1)

    w_in = by_head(window_keys, window_values)
    c_in = by_head(cache_keys, cache_values)
    slashes, verts = slash_offsets.shape[1], vertical_blocks.shape[1]
    keys = (slashes + verts) * BLOCK
    any_spec = pl.BlockSpec(memory_space=pl.ANY)
    smem = pl.BlockSpec(memory_space=pltpu.SMEM)
    dma = pltpu.SemaphoreType.DMA
    out = pl.pallas_call(
        functools.partial(kernel, n, members, heads, slashes, verts),
        out_shape=jax.ShapeDtypeStruct((head_count, span, dim), jnp.bfloat16),
        in_specs=[smem, smem, any_spec, any_spec, any_spec],
        out_specs=any_spec,
        scratch_shapes=[
            pltpu.VMEM((heads, members * span, dim), jnp.bfloat16),
            pltpu.VMEM((2, n * span // BLOCK, BLOCK, dim), jnp.bfloat16),
            pltpu.VMEM((2, n * cspan // BLOCK, BLOCK, dim), jnp.bfloat16),
            pltpu.VMEM((heads, members * span, dim), jnp.bfloat16),
            dma((n,)), dma((n,)), dma((n,)), dma((n,)),
            dma((heads, members)), dma((heads, members)),
            dma((heads, members)), dma((heads, members)),
            dma((3 + heads,)),
        ],
        compiler_params=pltpu.CompilerParams(
            collective_id=0, has_side_effects=True, vmem_limit_bytes=48 * 1024 * 1024
        ),
        cost_estimate=pl.CostEstimate(
            flops=4 * heads * members * span * keys * dim,
            bytes_accessed=16 * heads * members * span * dim,
            transcendentals=heads * members * span * keys,
        ),
    )(slash_offsets, vertical_blocks, q_in, w_in, c_in)
    return jnp.transpose(out, (1, 0, 2))


def solution(mesh):
    rows = P(("grp", "seq"), None, None)
    placed = (rows, rows, rows, rows, rows, P("grp", None), P("grp", None))
    return jax.shard_map(body, mesh=mesh, in_specs=placed, out_specs=rows, check_vma=False)
```

```python
import functools
import math

import jax
import jax.numpy as jnp
from jax import lax
from jax.experimental import pallas as pl
from jax.experimental.pallas import tpu as pltpu
from jax.sharding import PartitionSpec as P

BLOCK = 64
QUAD = 4
UNROLL = 4
LOG2E = 1.4426950408889634


def slash_part(q, block, row, offs_ref, w_s, lane_row, slashes, factor):
    pieces = []
    for c in range(slashes):
        offset = offs_ref[row, c]
        pieces.append((jnp.maximum(block - offset, 0), offset))
    chunks = [pieces[a : a + QUAD] for a in range(0, slashes, QUAD)]
    scores = []
    for chunk in chunks:
        keys = jnp.concatenate([w_s[0, index] for index, _ in chunk], axis=0)
        s = lax.dot_general(q, keys, (((1,), (1,)), ((), ())), preferred_element_type=jnp.float32)
        lane = lax.broadcasted_iota(jnp.int32, (1, s.shape[1]), 1)
        offsets = jnp.full((1, s.shape[1]), -1, jnp.int32)
        for a, (_, offset) in enumerate(chunk):
            offsets = jnp.where(lane // BLOCK == a, offset, offsets)
        limits = jnp.where(offsets > block, -4 * BLOCK, 4 * BLOCK)
        limits = jnp.where(offsets == 0, 0, limits)
        scores.append(jnp.where(lane_row[:, : s.shape[1]] <= limits, s, -1e30))
    top = functools.reduce(jnp.maximum, [jnp.max(s, axis=1, keepdims=True) for s in scores])
    total = None
    mixed = None
    for chunk, s in zip(chunks, scores):
        weights = jnp.exp2((s - top) * factor)
        part = jnp.sum(weights, axis=1, keepdims=True)
        values = jnp.concatenate([w_s[1, index] for index, _ in chunk], axis=0)
        product = jnp.dot(
            weights.astype(jnp.bfloat16), values, preferred_element_type=jnp.float32
        )
        total = part if total is None else total + part
        mixed = product if mixed is None else mixed + product
    return top, total, mixed


def kernel(
    n, members, heads, slashes, verts,
    offs_ref, vert_ref, q_in, w_in, c_in, out,
    q_s, w_s, c_s, o_s, top_s, total_s, mixed_s,
    w_send, w_recv, c_send, c_recv, q_send, q_recv, o_send, o_recv, local_sem,
):
    me = lax.axis_index("seq")
    member = lax.rem(me, members)
    base = me - member
    span = q_in.shape[1]
    first_head = member * heads

    barrier = pltpu.get_barrier_semaphore()

    def greet(k, _):
        pl.semaphore_signal(
            barrier, inc=1, device_id={"seq": lax.rem(me + k, n)},
            device_id_type=pl.DeviceIdType.MESH,
        )
        return 0

    lax.fori_loop(1, n, greet, 0)

    def span_of(index, length):
        return pl.ds(pl.multiple_of(index * length, length), length)

    def blocks_of(index, ref):
        return pl.ds(index * ref.shape[2], ref.shape[2])

    own = [
        pltpu.make_async_copy(w_in.at[member], w_s.at[:, blocks_of(me, w_in)], local_sem.at[0]),
        pltpu.make_async_copy(c_in.at[member], c_s.at[:, blocks_of(me, c_in)], local_sem.at[1]),
        pltpu.make_async_copy(
            q_in.at[pl.ds(first_head, heads)], q_s.at[:, span_of(member, span), :], local_sem.at[2]
        ),
    ]
    for copy in own:
        copy.start()
    pl.semaphore_wait(barrier, n - 1)

    def remote(src, dst, send, recv, peer):
        return pltpu.make_async_remote_copy(
            src_ref=src, dst_ref=dst, send_sem=send, recv_sem=recv,
            device_id={"seq": peer}, device_id_type=pl.DeviceIdType.MESH,
        )

    def w_copy(peer, place):
        return remote(
            w_in.at[lax.rem(peer, members)], w_s.at[:, blocks_of(place, w_in)],
            w_send.at[peer], w_recv.at[place], peer,
        )

    def c_copy(peer, place):
        return remote(
            c_in.at[lax.rem(peer, members)], c_s.at[:, blocks_of(place, c_in)],
            c_send.at[peer], c_recv.at[place], peer,
        )

    def q_copy(head, peer, place):
        return remote(
            q_in.at[peer * heads + head], q_s.at[head, span_of(place, span), :],
            q_send.at[head, peer], q_recv.at[head, place], base + peer,
        )

    def o_copy(head, peer, place):
        return remote(
            o_s.at[head, span_of(peer, span), :], out.at[place * heads + head],
            o_send.at[head, peer], o_recv.at[head, place], base + peer,
        )

    def start_w(k, _):
        w_copy(lax.rem(me + k, n), me).start()
        return 0

    lax.fori_loop(1, n, start_w, 0)
    share = -(-(n - 1) // heads)

    def start_head(head, _):
        def start_q(k, _):
            q_copy(head, lax.rem(member + k, members), member).start()
            return 0

        def start_c(k, _):
            @pl.when(k < n)
            def _():
                c_copy(lax.rem(me + k, n), me).start()

            return 0

        lax.fori_loop(1, members, start_q, 0)
        lax.fori_loop(1 + head * share, 1 + (head + 1) * share, start_c, 0)
        return 0

    lax.fori_loop(0, heads, start_head, 0)

    for copy in own:
        copy.wait()

    def wait_w(k, _):
        other = lax.rem(me + k, n)
        w_copy(other, other).wait_recv()
        return 0

    lax.fori_loop(1, n, wait_w, 0)

    lane_row = lax.rem(
        lax.broadcasted_iota(jnp.int32, (BLOCK, QUAD * BLOCK), 1), BLOCK
    ) - lax.broadcasted_iota(jnp.int32, (BLOCK, QUAD * BLOCK), 0)
    blocks = members * span // BLOCK
    first_block = (base * span) // BLOCK

    factor = LOG2E / math.sqrt(q_s.shape[-1])

    def slash_head(head, _):
        def wait_q(k, _):
            other = lax.rem(member + k, members)
            q_copy(head, other, other).wait_recv()
            return 0

        lax.fori_loop(1, members, wait_q, 0)

        def some_blocks(step, _):
            for part in range(UNROLL):
                local = step * UNROLL + part
                place = pl.ds(pl.multiple_of(local * BLOCK, BLOCK), BLOCK)
                top, total, mixed = slash_part(
                    q_s[head, place, :], first_block + local, first_head + head,
                    offs_ref, w_s, lane_row, slashes, factor,
                )
                top_s[head, place, :] = jnp.broadcast_to(top, mixed.shape)
                total_s[head, place, :] = jnp.broadcast_to(total, mixed.shape)
                mixed_s[head, place, :] = mixed
            return 0

        lax.fori_loop(0, blocks // UNROLL, some_blocks, 0)
        return 0

    lax.fori_loop(0, heads, slash_head, 0)

    def wait_c(k, _):
        other = lax.rem(me + k, n)
        c_copy(other, other).wait_recv()
        return 0

    lax.fori_loop(1, n, wait_c, 0)
    tall = math.gcd(members * span, 4 * BLOCK)

    def vertical_head(head, _):
        row = first_head + head
        picks = [vert_ref[row, c] for c in range(verts)]
        keys = jnp.concatenate([c_s[0, pick] for pick in picks], axis=0)
        values = jnp.concatenate([c_s[1, pick] for pick in picks], axis=0)
        for step in range(members * span // tall):
            place = pl.ds(step * tall, tall)
            s = lax.dot_general(
                q_s[head, place, :], keys, (((1,), (1,)), ((), ())),
                preferred_element_type=jnp.float32,
            )
            before = top_s[head, place, :]
            top = jnp.maximum(before, jnp.max(s, axis=1, keepdims=True))
            scale = jnp.exp2((before - top) * factor)
            weights = jnp.exp2((s - top[:, :1]) * factor)
            total = total_s[head, place, :] * scale + jnp.sum(weights, axis=1, keepdims=True)
            product = jnp.dot(
                weights.astype(jnp.bfloat16), values, preferred_element_type=jnp.float32
            )
            mixed = mixed_s[head, place, :] * scale + product
            o_s[head, place, :] = (mixed / total).astype(jnp.bfloat16)

        def start_o(k, _):
            o_copy(head, lax.rem(member + k, members), member).start()
            return 0

        lax.fori_loop(1, members, start_o, 0)
        pltpu.make_async_copy(
            o_s.at[head, span_of(member, span), :], out.at[first_head + head],
            local_sem.at[3 + head],
        ).start()
        return 0

    lax.fori_loop(0, heads, vertical_head, 0)

    def finish_kv(k, _):
        peer = lax.rem(me + k, n)
        w_copy(peer, me).wait_send()
        c_copy(peer, me).wait_send()
        return 0

    lax.fori_loop(1, n, finish_kv, 0)

    def finish_head(head, _):
        def each(k, _):
            other = lax.rem(member + k, members)
            q_copy(head, other, member).wait_send()
            o_copy(head, other, member).wait_send()
            o_copy(head, other, other).wait_recv()
            return 0

        lax.fori_loop(1, members, each, 0)
        pltpu.make_async_copy(
            o_s.at[head, span_of(member, span), :], out.at[first_head + head],
            local_sem.at[3 + head],
        ).wait()
        return 0

    lax.fori_loop(0, heads, finish_head, 0)


def body(queries, window_keys, window_values, cache_keys, cache_values, vertical_blocks, slash_offsets):
    n = lax.axis_size("seq")
    span, head_count, dim = queries.shape
    members = window_keys.shape[1]
    cspan = cache_keys.shape[0]
    heads = head_count // members
    q_in = jnp.transpose(queries, (1, 0, 2))

    def by_head(keys, values):
        both = [jnp.transpose(a, (1, 0, 2)).reshape(members, -1, BLOCK, dim) for a in (keys, values)]
        return jnp.stack(both, axis=1)

    w_in = by_head(window_keys, window_values)
    c_in = by_head(cache_keys, cache_values)
    slashes, verts = slash_offsets.shape[1], vertical_blocks.shape[1]
    keys = (slashes + verts) * BLOCK
    any_spec = pl.BlockSpec(memory_space=pl.ANY)
    smem = pl.BlockSpec(memory_space=pltpu.SMEM)
    dma = pltpu.SemaphoreType.DMA
    out = pl.pallas_call(
        functools.partial(kernel, n, members, heads, slashes, verts),
        out_shape=jax.ShapeDtypeStruct((head_count, span, dim), jnp.bfloat16),
        in_specs=[smem, smem, any_spec, any_spec, any_spec],
        out_specs=any_spec,
        scratch_shapes=[
            pltpu.VMEM((heads, members * span, dim), jnp.bfloat16),
            pltpu.VMEM((2, n * span // BLOCK, BLOCK, dim), jnp.bfloat16),
            pltpu.VMEM((2, n * cspan // BLOCK, BLOCK, dim), jnp.bfloat16),
            pltpu.VMEM((heads, members * span, dim), jnp.bfloat16),
            pltpu.VMEM((heads, members * span, dim), jnp.float32),
            pltpu.VMEM((heads, members * span, dim), jnp.float32),
            pltpu.VMEM((heads, members * span, dim), jnp.float32),
            dma((n,)), dma((n,)), dma((n,)), dma((n,)),
            dma((heads, members)), dma((heads, members)),
            dma((heads, members)), dma((heads, members)),
            dma((3 + heads,)),
        ],
        compiler_params=pltpu.CompilerParams(
            collective_id=0, has_side_effects=True, vmem_limit_bytes=48 * 1024 * 1024
        ),
        cost_estimate=pl.CostEstimate(
            flops=4 * heads * members * span * keys * dim,
            bytes_accessed=16 * heads * members * span * dim,
            transcendentals=heads * members * span * keys,
        ),
    )(slash_offsets, vertical_blocks, q_in, w_in, c_in)
    return jnp.transpose(out, (1, 0, 2))


def solution(mesh):
    rows = P(("grp", "seq"), None, None)
    placed = (rows, rows, rows, rows, rows, P("grp", None), P("grp", None))
    return jax.shard_map(body, mesh=mesh, in_specs=placed, out_specs=rows, check_vma=False)
```

```python
import functools
import math

import jax
import jax.numpy as jnp
from jax import lax
from jax.experimental import pallas as pl
from jax.experimental.pallas import tpu as pltpu
from jax.sharding import PartitionSpec as P

BLOCK = 64
QUAD = 4
UNROLL = 4
LOG2E = 1.4426950408889634


def slash_part(q, block, row, offs_ref, w_s, lane_row, slashes, factor):
    pieces = []
    for c in range(slashes):
        offset = offs_ref[row, c]
        pieces.append((jnp.maximum(block - offset, 0), offset))
    chunks = [pieces[a : a + QUAD] for a in range(0, slashes, QUAD)]
    scores = []
    for chunk in chunks:
        keys = jnp.concatenate([w_s[0, index] for index, _ in chunk], axis=0)
        s = lax.dot_general(q, keys, (((1,), (1,)), ((), ())), preferred_element_type=jnp.float32)
        lane = lax.broadcasted_iota(jnp.int32, (1, s.shape[1]), 1)
        offsets = jnp.full((1, s.shape[1]), -1, jnp.int32)
        for a, (_, offset) in enumerate(chunk):
            offsets = jnp.where(lane // BLOCK == a, offset, offsets)
        limits = jnp.where(offsets > block, -4 * BLOCK, 4 * BLOCK)
        limits = jnp.where(offsets == 0, 0, limits)
        scores.append(jnp.where(lane_row[:, : s.shape[1]] <= limits, s, -1e30))
    top = functools.reduce(jnp.maximum, [jnp.max(s, axis=1, keepdims=True) for s in scores])
    total = None
    mixed = None
    for chunk, s in zip(chunks, scores):
        weights = jnp.exp2((s - top) * factor)
        part = jnp.sum(weights, axis=1, keepdims=True)
        values = jnp.concatenate([w_s[1, index] for index, _ in chunk], axis=0)
        product = jnp.dot(
            weights.astype(jnp.bfloat16), values, preferred_element_type=jnp.float32
        )
        total = part if total is None else total + part
        mixed = product if mixed is None else mixed + product
    return top, total, mixed


def kernel(
    n, members, heads, slashes, verts,
    offs_ref, vert_ref, q_in, w_in, c_in, out,
    q_s, w_s, c_s, o_s, top_s, total_s, mixed_s,
    w_send, w_recv, c_send, c_recv, q_send, q_recv, o_send, o_recv, local_sem,
):
    me = lax.axis_index("seq")
    member = lax.rem(me, members)
    base = me - member
    stride = 7 if math.gcd(7, n) == 1 else 1
    span = q_in.shape[1]
    first_head = member * heads

    barrier = pltpu.get_barrier_semaphore()

    def greet(k, _):
        pl.semaphore_signal(
            barrier, inc=1, device_id={"seq": lax.rem(me + k * stride, n)},
            device_id_type=pl.DeviceIdType.MESH,
        )
        return 0

    lax.fori_loop(1, n, greet, 0)

    def span_of(index, length):
        return pl.ds(pl.multiple_of(index * length, length), length)

    def blocks_of(index, ref):
        return pl.ds(index * ref.shape[2], ref.shape[2])

    own = [
        pltpu.make_async_copy(w_in.at[member], w_s.at[:, blocks_of(me, w_in)], local_sem.at[0]),
        pltpu.make_async_copy(c_in.at[member], c_s.at[:, blocks_of(me, c_in)], local_sem.at[1]),
        pltpu.make_async_copy(
            q_in.at[pl.ds(first_head, heads)], q_s.at[:, span_of(member, span), :], local_sem.at[2]
        ),
    ]
    for copy in own:
        copy.start()
    pl.semaphore_wait(barrier, n - 1)

    def remote(src, dst, send, recv, peer):
        return pltpu.make_async_remote_copy(
            src_ref=src, dst_ref=dst, send_sem=send, recv_sem=recv,
            device_id={"seq": peer}, device_id_type=pl.DeviceIdType.MESH,
        )

    def w_copy(peer, place):
        return remote(
            w_in.at[lax.rem(peer, members)], w_s.at[:, blocks_of(place, w_in)],
            w_send.at[peer], w_recv.at[place], peer,
        )

    def c_copy(peer, place):
        return remote(
            c_in.at[lax.rem(peer, members)], c_s.at[:, blocks_of(place, c_in)],
            c_send.at[peer], c_recv.at[place], peer,
        )

    def q_copy(head, peer, place):
        return remote(
            q_in.at[peer * heads + head], q_s.at[head, span_of(place, span), :],
            q_send.at[head, peer], q_recv.at[head, place], base + peer,
        )

    def o_copy(head, peer, place):
        return remote(
            o_s.at[head, span_of(peer, span), :], out.at[place * heads + head],
            o_send.at[head, peer], o_recv.at[head, place], base + peer,
        )

    def start_w(k, _):
        w_copy(lax.rem(me + k * stride, n), me).start()
        return 0

    share = -(-(n - 1) // heads)

    def start_head(head, _):
        def start_q(k, _):
            q_copy(head, lax.rem(member + k, members), member).start()
            return 0

        def start_c(k, _):
            @pl.when(k < n)
            def _():
                c_copy(lax.rem(me + k * stride, n), me).start()

            return 0

        lax.fori_loop(1 + head * share, 1 + (head + 1) * share, start_c, 0)
        return 0

    lax.fori_loop(1, n, start_w, 0)

    def start_qs(head, _):
        def start_q(k, _):
            q_copy(head, lax.rem(member + k, members), member).start()
            return 0

        lax.fori_loop(1, members, start_q, 0)
        return 0

    lax.fori_loop(0, heads, start_qs, 0)
    lax.fori_loop(0, heads, start_head, 0)

    for copy in own:
        copy.wait()

    def wait_w(k, _):
        other = lax.rem(me + k * stride, n)
        w_copy(other, other).wait_recv()
        return 0

    lax.fori_loop(1, n, wait_w, 0)

    lane_row = lax.rem(
        lax.broadcasted_iota(jnp.int32, (BLOCK, QUAD * BLOCK), 1), BLOCK
    ) - lax.broadcasted_iota(jnp.int32, (BLOCK, QUAD * BLOCK), 0)
    blocks = members * span // BLOCK
    first_block = (base * span) // BLOCK

    factor = LOG2E / math.sqrt(q_s.shape[-1])

    def slash_head(head, _):
        def wait_q(k, _):
            other = lax.rem(member + k, members)
            q_copy(head, other, other).wait_recv()
            return 0

        lax.fori_loop(1, members, wait_q, 0)

        def some_blocks(step, _):
            for part in range(UNROLL):
                local = step * UNROLL + part
                place = pl.ds(pl.multiple_of(local * BLOCK, BLOCK), BLOCK)
                top, total, mixed = slash_part(
                    q_s[head, place, :], first_block + local, first_head + head,
                    offs_ref, w_s, lane_row, slashes, factor,
                )
                top_s[head, place, :] = jnp.broadcast_to(top, mixed.shape)
                total_s[head, place, :] = jnp.broadcast_to(total, mixed.shape)
                mixed_s[head, place, :] = mixed
            return 0

        lax.fori_loop(0, blocks // UNROLL, some_blocks, 0)
        return 0

    lax.fori_loop(0, heads, slash_head, 0)

    def wait_c(k, _):
        other = lax.rem(me + k * stride, n)
        c_copy(other, other).wait_recv()
        return 0

    lax.fori_loop(1, n, wait_c, 0)
    tall = math.gcd(members * span, 4 * BLOCK)

    def vertical_head(head, _):
        row = first_head + head
        picks = [vert_ref[row, c] for c in range(verts)]
        keys = jnp.concatenate([c_s[0, pick] for pick in picks], axis=0)
        values = jnp.concatenate([c_s[1, pick] for pick in picks], axis=0)
        for step in range(members * span // tall):
            place = pl.ds(step * tall, tall)
            s = lax.dot_general(
                q_s[head, place, :], keys, (((1,), (1,)), ((), ())),
                preferred_element_type=jnp.float32,
            )
            before = top_s[head, place, :]
            top = jnp.maximum(before, jnp.max(s, axis=1, keepdims=True))
            scale = jnp.exp2((before - top) * factor)
            weights = jnp.exp2((s - top[:, :1]) * factor)
            total = total_s[head, place, :] * scale + jnp.sum(weights, axis=1, keepdims=True)
            product = jnp.dot(
                weights.astype(jnp.bfloat16), values, preferred_element_type=jnp.float32
            )
            mixed = mixed_s[head, place, :] * scale + product
            o_s[head, place, :] = (mixed / total).astype(jnp.bfloat16)

        def start_o(k, _):
            o_copy(head, lax.rem(member + k, members), member).start()
            return 0

        lax.fori_loop(1, members, start_o, 0)
        pltpu.make_async_copy(
            o_s.at[head, span_of(member, span), :], out.at[first_head + head],
            local_sem.at[3 + head],
        ).start()
        return 0

    lax.fori_loop(0, heads, vertical_head, 0)

    def finish_kv(k, _):
        peer = lax.rem(me + k * stride, n)
        w_copy(peer, me).wait_send()
        c_copy(peer, me).wait_send()
        return 0

    lax.fori_loop(1, n, finish_kv, 0)

    def finish_head(head, _):
        def each(k, _):
            other = lax.rem(member + k, members)
            q_copy(head, other, member).wait_send()
            o_copy(head, other, member).wait_send()
            o_copy(head, other, other).wait_recv()
            return 0

        lax.fori_loop(1, members, each, 0)
        pltpu.make_async_copy(
            o_s.at[head, span_of(member, span), :], out.at[first_head + head],
            local_sem.at[3 + head],
        ).wait()
        return 0

    lax.fori_loop(0, heads, finish_head, 0)


def body(queries, window_keys, window_values, cache_keys, cache_values, vertical_blocks, slash_offsets):
    n = lax.axis_size("seq")
    span, head_count, dim = queries.shape
    members = window_keys.shape[1]
    cspan = cache_keys.shape[0]
    heads = head_count // members
    q_in = jnp.transpose(queries, (1, 0, 2))

    def by_head(keys, values):
        both = [jnp.transpose(a, (1, 0, 2)).reshape(members, -1, BLOCK, dim) for a in (keys, values)]
        return jnp.stack(both, axis=1)

    w_in = by_head(window_keys, window_values)
    c_in = by_head(cache_keys, cache_values)
    slashes, verts = slash_offsets.shape[1], vertical_blocks.shape[1]
    keys = (slashes + verts) * BLOCK
    any_spec = pl.BlockSpec(memory_space=pl.ANY)
    smem = pl.BlockSpec(memory_space=pltpu.SMEM)
    dma = pltpu.SemaphoreType.DMA
    out = pl.pallas_call(
        functools.partial(kernel, n, members, heads, slashes, verts),
        out_shape=jax.ShapeDtypeStruct((head_count, span, dim), jnp.bfloat16),
        in_specs=[smem, smem, any_spec, any_spec, any_spec],
        out_specs=any_spec,
        scratch_shapes=[
            pltpu.VMEM((heads, members * span, dim), jnp.bfloat16),
            pltpu.VMEM((2, n * span // BLOCK, BLOCK, dim), jnp.bfloat16),
            pltpu.VMEM((2, n * cspan // BLOCK, BLOCK, dim), jnp.bfloat16),
            pltpu.VMEM((heads, members * span, dim), jnp.bfloat16),
            pltpu.VMEM((heads, members * span, dim), jnp.float32),
            pltpu.VMEM((heads, members * span, dim), jnp.float32),
            pltpu.VMEM((heads, members * span, dim), jnp.float32),
            dma((n,)), dma((n,)), dma((n,)), dma((n,)),
            dma((heads, members)), dma((heads, members)),
            dma((heads, members)), dma((heads, members)),
            dma((3 + heads,)),
        ],
        compiler_params=pltpu.CompilerParams(
            collective_id=0, has_side_effects=True, vmem_limit_bytes=48 * 1024 * 1024
        ),
        cost_estimate=pl.CostEstimate(
            flops=4 * heads * members * span * keys * dim,
            bytes_accessed=16 * heads * members * span * dim,
            transcendentals=heads * members * span * keys,
        ),
    )(slash_offsets, vertical_blocks, q_in, w_in, c_in)
    return jnp.transpose(out, (1, 0, 2))


def solution(mesh):
    rows = P(("grp", "seq"), None, None)
    placed = (rows, rows, rows, rows, rows, P("grp", None), P("grp", None))
    return jax.shard_map(body, mesh=mesh, in_specs=placed, out_specs=rows, check_vma=False)
```
